32 devices in a mesh: space: 8 (over z, x), segment: 4 (over y, core).
Axes of the slice: x: 2, y: 2, z: 4, core: 2. Of those that a mesh axis runs over, the one named last changes fastest.
Arguments:
- field: bfloat16 [4, 64, 8, 8, 128], P(None, 'space'), may hold values from -6 to 6
- depth_kernel: bfloat16 [8, 49, 128], P('segment'), may hold values from -0.875 to 0.875
- depth_bias: bfloat16 [8, 128], P('segment'), may hold values from -3 to 3
- norm_gain: bfloat16 [8, 128], P('segment'), may hold values from 0.099609375 to 1.8984375
- up_weight: bfloat16 [8, 128, 512], P('segment'), may hold values from -0.5 to 0.5
- up_bias: bfloat16 [8, 512], P('segment'), may hold values from -3 to 3
- down_weight: bfloat16 [8, 512, 128], P('segment'), may hold values from -0.25 to 0.25
- scale_exponent: int32 [8, 128], P('segment'), may hold values from -3 to 1
- live_count: int32 [8], P('space'), may hold values from 4 to 8, as said below
- neighbours: int32 [64, 8], P('space'), may hold values from -1 to 63, as said below
- rotations: int32 [64, 8], P('space'), may hold values from 0 to 3
Outputs:
- boundary: bfloat16 [4, 4, 64, 8, 8, 128], P('segment', None, 'space')
The draws below stay inside these ranges and needn't reach their ends.
Inputs may be any that keep to these rules, and one draw needn't show every extreme that they name: `live_count`: at least one index of space holds 8 land patches. `neighbours`: every entry of a live slot is -1, a live slot of the same index of space, one of the first 1 slots of the next index along space, or one of the last 1 slots of the previous one, counted around the cycle; entries of slots that are not live are -1.
All inputs are finite; a program needn't handle non-finite values.
Results may differ from the reference program's by a relative error of at most 0.03.
Values may be sent and summed in bfloat16 or wider, within the bound.
A program may use at most 64 MiB of HBM per device.

```python
import jax
import jax.numpy as jnp
from jax import lax

C = 128
HID = 512
KS = 7
PS = 8
BPS = 2
EDGE = 1
PD = 8
MEMBERS = 4
NPATCH = 64
BLOCKS = 8


def land_counts(key):
    inner = jax.random.fold_in(key, 11)
    first, second = jax.random.split(inner)
    devices = NPATCH // PD
    lowest = max(2 * EDGE, PD // 2)
    counts = jax.random.randint(first, (devices,), lowest, PD + 1)
    fullest = jax.random.randint(second, (), 0, devices)
    return counts.at[fullest].set(PD).astype(jnp.int32)


def draw_live_count(key, part):
    return land_counts(key)


def draw_neighbours(key, part):
    counts = land_counts(key)
    devices = NPATCH // PD
    inner = jax.random.fold_in(key, 23)
    first, second, third, fourth = jax.random.split(inner, 4)
    slots = jnp.arange(NPATCH, dtype=jnp.int32)
    owner = slots // PD
    within = slots % PD
    offset = jax.random.randint(first, (NPATCH, 8), -1, 2)
    target = (owner[:, None] + offset) % devices
    pick = jax.random.randint(second, (NPATCH, 8), 0, 1 << 20)
    own_count = counts[owner][:, None]
    ranked = pick % own_count
    own_pos = jnp.where(ranked < own_count - EDGE, ranked, ranked + PD - own_count)
    edge_pick = jax.random.randint(fourth, (NPATCH, 8), 0, EDGE)
    next_pos = edge_pick
    prev_pos = PD - EDGE + edge_pick
    position = jnp.where(offset == 0, own_pos, jnp.where(offset == 1, next_pos, prev_pos))
    linked = target * PD + position
    ocean = jax.random.randint(third, (NPATCH, 8), 0, 4) == 0
    alive = (within < counts[owner] - EDGE) | (within >= PD - EDGE)
    return jnp.where(ocean | jnp.logical_not(alive)[:, None], -1, linked).astype(jnp.int32)


def place_ends(array, rng, least, largest):
    longest = array.shape.index(max(array.shape))
    spots = []
    for shift in (0, 1):
        where = [jax.random.randint(jax.random.fold_in(rng, axis), (), 0, length) for axis, length in enumerate(array.shape)]
        where[longest] = (where[longest] + shift) % array.shape[longest]
        spots.append(tuple(where))
    return array.at[spots[0]].set(least).at[spots[1]].set(largest)


def steps_of(rng, shape, cuts, low, largest):
    def one(dim, shards_of):
        steps = jax.random.uniform(jax.random.fold_in(jax.random.fold_in(rng, 6), dim), (shards_of,), jnp.float32, low / len(cuts), largest / len(cuts))
        return jnp.repeat(jnp.exp(steps), shape[dim] // shards_of).reshape((-1,) + (1,) * (len(shape) - dim - 1))

    loudness = one(*cuts[0])
    for cut in cuts[1:]:
        loudness = loudness * one(*cut)
    return loudness


def bell_draw(stream_key, shape, deviation, reach, cuts=(), kind=jnp.bfloat16):
    level = steps_of(stream_key, shape, cuts, -0.22, 0.18) if cuts else 1.0
    drawn = jax.random.normal(stream_key, shape, jnp.float32) * deviation * level
    return jnp.minimum(jnp.maximum(drawn, -reach), reach).astype(kind)


def setup_inputs(seed: int = 0) -> dict:
    arg_keys = jax.random.split(jax.random.key(seed), 12)
    return {
        "field": bell_draw(arg_keys[0], (MEMBERS, NPATCH, PS, PS, C), 1.0, 6.0, ((1, 8),)),
        "depth_kernel": bell_draw(arg_keys[1], (BLOCKS, KS * KS, C), (KS * KS) ** -0.5, 0.875, ((0, 4),)),
        "depth_bias": bell_draw(arg_keys[2], (BLOCKS, C), 0.5, 3.0, ((0, 4),)),
        "norm_gain": jnp.clip(1.0 + 0.18 * jax.random.normal(arg_keys[3], (BLOCKS, C), jnp.float32), 0.099609375, 1.8984375).astype(jnp.bfloat16),
        "up_weight": bell_draw(arg_keys[4], (BLOCKS, C, HID), C ** -0.5, 0.5, ((0, 4),)),
        "up_bias": bell_draw(arg_keys[5], (BLOCKS, HID), 0.5, 3.0, ((0, 4),)),
        "down_weight": bell_draw(arg_keys[6], (BLOCKS, HID, C), HID ** -0.5, 0.25, ((0, 4),)),
        "scale_exponent": place_ends(jax.random.randint(arg_keys[7], (BLOCKS, C), -3, 2), jax.random.fold_in(arg_keys[7], 1), -3, 1).astype(jnp.int32),
        "live_count": draw_live_count(jax.random.fold_in(arg_keys[11], 71), 0),
        "neighbours": draw_neighbours(jax.random.fold_in(arg_keys[11], 71), 0),
        "rotations": place_ends(jax.random.randint(arg_keys[10], (NPATCH, 8), 0, 4), jax.random.fold_in(arg_keys[10], 1), 0, 3).astype(jnp.int32),
    }


def rotate_tiles(tiles, turns):
    result = tiles
    for quarter in (1, 2, 3):
        turned = jnp.rot90(tiles, quarter, axes=(2, 3))
        result = jnp.where((turns == quarter)[:, :, None, None, None], turned, result)
    return result

def assemble(tiles, center, margin):
    upper = jnp.concatenate([tiles[:, 0, -margin:, -margin:], tiles[:, 1, -margin:, :], tiles[:, 2, -margin:, :margin]], axis=2)
    middle = jnp.concatenate([tiles[:, 3, :, -margin:], center, tiles[:, 4, :, :margin]], axis=2)
    lower = jnp.concatenate([tiles[:, 5, :margin, -margin:], tiles[:, 6, :margin, :], tiles[:, 7, :margin, :margin]], axis=2)
    return jnp.concatenate([upper, middle, lower], axis=1)

def apply_block(state, tiles, live, kernel, kernel_bias, gain, weight_up, bias_up, weight_down, gamma):
    margin = KS // 2
    side = state.shape[1]
    chans = state.shape[3]
    extended = assemble(tiles, state, margin)
    total = jnp.zeros(state.shape, jnp.float32) + kernel_bias.astype(jnp.float32)
    for row in range(KS):
        for column in range(KS):
            window = extended[:, row:row + side, column:column + side, :].astype(jnp.float32)
            total = total + window * kernel[row * KS + column].astype(jnp.float32)
    mean = lax.optimization_barrier(jnp.mean(total, axis=-1, keepdims=True))
    centred = total - mean
    variance = lax.optimization_barrier(jnp.mean(centred * centred, axis=-1, keepdims=True))
    normed = (centred * lax.rsqrt(variance + 1e-06) * gain.astype(jnp.float32)).astype(jnp.bfloat16)
    flat = normed.reshape(-1, chans)
    hidden = jax.nn.gelu(jnp.dot(flat, weight_up, preferred_element_type=jnp.float32) + bias_up.astype(jnp.float32), approximate=False).astype(jnp.bfloat16)
    branch = jnp.dot(hidden, weight_down, preferred_element_type=jnp.float32).reshape(state.shape)
    return ((state.astype(jnp.float32) + gamma * branch) * live[:, None, None, None]).astype(jnp.bfloat16)

def reference(field, depth_kernel, depth_bias, norm_gain, up_weight, up_bias, down_weight, scale_exponent, live_count, neighbours, rotations):
    slots = jnp.arange(NPATCH, dtype=jnp.int32)
    within = slots % PD
    owned = live_count[slots // PD]
    live = ((within < owned - EDGE) | (within >= PD - EDGE)).astype(jnp.float32)
    gamma = jnp.exp2(scale_exponent.astype(jnp.float32) * 0.5)
    links = jnp.where(neighbours < 0, NPATCH, neighbours).astype(jnp.int32)
    sections = []
    for member in range(MEMBERS):
        state = field[member]
        results = []
        for block in range(BLOCKS):
            padded = jnp.concatenate([state, jnp.zeros((1,) + state.shape[1:], state.dtype)], axis=0)
            tiles = rotate_tiles(padded[links], rotations)
            state = apply_block(state, tiles, live, depth_kernel[block], depth_bias[block], norm_gain[block], up_weight[block], up_bias[block], down_weight[block], gamma[block])
            if (block + 1) % BPS == 0:
                results.append(state)
        sections.append(jnp.stack(results, axis=0))
    return jnp.stack(sections, axis=1)
```

```python
import functools

import jax
import jax.numpy as jnp
import numpy as np
from jax import lax
from jax.experimental import pallas as pl
from jax.experimental.pallas import tpu as pltpu
from jax.sharding import PartitionSpec as P

KS = 7
BPS = 2
EDGE = 1
MARGIN = KS // 2
PS = 8
CELLS = PS * PS
EXT = PS + 2 * MARGIN
PITCH = 15
ROWS = 216
MESH = pl.DeviceIdType.MESH

BIAS = KS * KS
GAIN = BIAS + 1
SCALE = GAIN + 1
UP_BIAS = SCALE + 1


def tables():
    direction = np.full((ROWS,), -1, np.int32)
    source = np.zeros((4, ROWS), np.int32)
    last = PS - 1
    for j in range(EXT):
        for i in range(EXT):
            band_i = 0 if i < MARGIN else (1 if i < MARGIN + PS else 2)
            band_j = 0 if j < MARGIN else (1 if j < MARGIN + PS else 2)
            u = (i + PS - MARGIN) % PS
            v = (j + PS - MARGIN) % PS
            d = ((0, 1, 2), (3, 8, 4), (5, 6, 7))[band_i][band_j]
            r = j * PITCH + i
            direction[r] = d
            turned = ((u, v), (v, last - u), (last - u, last - v), (last - v, u))
            for k, (p, q) in enumerate(turned):
                source[k, r] = p * PS + q
    return direction, source


def routing(neighbours, rotations):
    count = neighbours.shape[0]
    place = lax.axis_index("space")
    devices = lax.axis_size("space")
    direction, source = tables()
    relative = (neighbours // count - place) % devices
    within = neighbours % count
    slot = jnp.where(relative == 0, within, jnp.where(relative == 1, count + 1, count))
    slot = jnp.where(neighbours < 0, -1, slot)
    own = jnp.arange(count, dtype=jnp.int32)[:, None]
    slot9 = [slot[:, d : d + 1] for d in range(8)] + [own]
    turn9 = [rotations[:, d : d + 1] for d in range(8)] + [jnp.zeros_like(own)]
    link = jnp.full((count, ROWS), -1, jnp.int32)
    turn = jnp.zeros((count, ROWS), jnp.int32)
    for d in range(9):
        here = jnp.asarray(direction == d)[None]
        link = jnp.where(here, slot9[d], link)
        turn = jnp.where(here, turn9[d], turn)
    cell = jnp.zeros((count, ROWS), jnp.int32)
    for k in range(4):
        cell = jnp.where(turn == k, jnp.asarray(source[k])[None], cell)
    target = jnp.where(link < 0, -1, link * CELLS + cell)
    columns = lax.broadcasted_iota(jnp.int32, (count, ROWS, (count + 2) * CELLS), 2)
    return (target[:, :, None] == columns).astype(jnp.bfloat16)


def gelu(x):
    return 0.5 * x * (1.0 + lax.erf(x * np.float32(0.5**0.5)))


def kernel(
    segments,
    devices,
    blocks,
    field,
    taps,
    bias,
    gain,
    up,
    up_bias,
    down,
    scale,
    live_count,
    route,
    out,
    win,
    ups,
    downs,
    small,
    ext,
    loc_sem,
    own_sem,
    w_recv,
    fwd_sem,
    h_send,
    h_recv,
    o_send,
    o_recv,
):
    space = lax.axis_index("space")
    me = lax.axis_index("segment")
    count = live_rows = win.shape[1] // CELLS - 2
    rows = count * CELLS
    after = lax.rem(space + 1, devices)
    before = lax.rem(space + devices - 1, devices)
    core = lax.rem(me, 2)
    pair = me // 2
    partner = pair * 2 + (1 - core)
    pairs = segments // 2
    mine = me * BPS

    start_field = pltpu.make_async_copy(field.at[me], win.at[0, pl.ds(0, rows)], loc_sem.at[0])
    start_field.start()
    own_up = pltpu.make_async_copy(up, ups.at[pl.ds(mine, BPS)], loc_sem.at[1])
    own_up.start()
    own_down = pltpu.make_async_copy(down, downs.at[pl.ds(mine, BPS)], loc_sem.at[2])
    own_down.start()
    hid = up_bias.shape[1]
    chans = up.shape[1]
    for k in range(BPS):
        small[mine + k, 0 : KS * KS, :] = taps[k].astype(jnp.float32)
        small[mine + k, BIAS : BIAS + 1, :] = bias[k : k + 1, :].astype(jnp.float32)
        small[mine + k, GAIN : GAIN + 1, :] = gain[k : k + 1, :].astype(jnp.float32)
        small[mine + k, SCALE : SCALE + 1, :] = jnp.exp2(
            scale[k : k + 1, :].astype(jnp.float32) * 0.5
        )
        for q in range(hid // chans):
            small[mine + k, UP_BIAS + q : UP_BIAS + q + 1, :] = up_bias[
                k : k + 1, q * chans : (q + 1) * chans
            ].astype(jnp.float32)

    barrier = pltpu.get_barrier_semaphore()
    for step in range(1, segments):
        pl.semaphore_signal(
            barrier,
            inc=1,
            device_id=(space, lax.rem(me + step, segments)),
            device_id_type=MESH,
        )
    for side in (before, after):
        pl.semaphore_signal(barrier, inc=1, device_id=(side, me), device_id_type=MESH)
    pl.semaphore_wait(barrier, segments + 1)

    def halo(b, side):
        if side == 0:
            src = win.at[b, pl.ds(rows - CELLS, CELLS)]
            dst, to = win.at[b, pl.ds(rows, CELLS)], after
        else:
            src = win.at[b, pl.ds(0, CELLS)]
            dst, to = win.at[b, pl.ds(rows + CELLS, CELLS)], before
        return pltpu.make_async_remote_copy(
            src_ref=src,
            dst_ref=dst,
            send_sem=h_send.at[b, side],
            recv_sem=h_recv.at[b, side],
            device_id=(to, me),
            device_id_type=MESH,
        )

    def piece(kind, b, to, send_sem):
        ref = (small, ups, downs)[kind].at[b]
        return pltpu.make_async_remote_copy(
            src_ref=ref,
            dst_ref=ref,
            send_sem=send_sem,
            recv_sem=w_recv.at[kind, b],
            device_id=(space, to),
            device_id_type=MESH,
        )

    def to_partner():
        return [
            piece(kind, mine + k, partner, own_sem.at[k, kind])
            for k in range(BPS)
            for kind in range(3)
        ]

    def to_pairs():
        copies = []
        for k in range(BPS):
            for step in range(1, pairs):
                other = lax.rem(pair + step, pairs) * 2
                at = 3 + (step - 1) * 4
                copies.append(piece(0, mine + k, other, own_sem.at[k, at]))
                copies.append(piece(0, mine + k, other + 1, own_sem.at[k, at + 1]))
                copies.append(piece(1, mine + k, other, own_sem.at[k, at + 2]))
                copies.append(piece(2, mine + k, other + 1, own_sem.at[k, at + 3]))
        return copies

    def forwarded(b, act):
        foreign = b // (2 * BPS) != pair

        @pl.when(jnp.logical_and(foreign, core == 0))
        def _():
            act(piece(1, b, partner, fwd_sem.at[b]))

        @pl.when(jnp.logical_and(foreign, core == 1))
        def _():
            act(piece(2, b, partner, fwd_sem.at[b]))

    def forward(b):
        def act(copy):
            copy.wait_recv()
            copy.start()

        forwarded(b, act)

    def arrive(b):
        owner = b // BPS
        foreign = b // (2 * BPS) != pair

        @pl.when(owner != me)
        def _():
            piece(0, b, partner, fwd_sem.at[b]).wait_recv()

        @pl.when(owner == partner)
        def _():
            piece(1, b, partner, fwd_sem.at[b]).wait_recv()
            piece(2, b, partner, fwd_sem.at[b]).wait_recv()

        @pl.when(jnp.logical_and(foreign, core == 0))
        def _():
            piece(2, b, partner, fwd_sem.at[b]).wait_recv()

        @pl.when(jnp.logical_and(foreign, core == 1))
        def _():
            piece(1, b, partner, fwd_sem.at[b]).wait_recv()

    def result(s):
        return win.at[BPS * (s + 1), pl.ds(0, rows)]

    def send_result(s):
        return pltpu.make_async_remote_copy(
            src_ref=result(s),
            dst_ref=out.at[me],
            send_sem=o_send.at[s],
            recv_sem=o_recv.at[me],
            device_id=(space, s),
            device_id_type=MESH,
        )

    def keep_result(s):
        return pltpu.make_async_copy(result(s), out.at[me], loc_sem.at[3])

    def convolve(b, g):
        ext[pl.ds(0, ROWS), :] = jnp.dot(route[g], win[b], preferred_element_type=jnp.float32)
        total = jnp.broadcast_to(small[b, BIAS : BIAS + 1, :][None], (PS, PS, chans))
        for e in range(KS):
            column = jnp.concatenate(
                [ext[pl.ds(e * PITCH + i, PS, stride=PITCH), :][None] for i in range(EXT)], axis=0
            )
            for a in range(KS):
                tap = small[b, a * KS + e : a * KS + e + 1, :][None]
                total = total + column[a : a + PS] * tap
        total = total.reshape(CELLS, chans)
        centred = total - jnp.mean(total, axis=-1, keepdims=True)
        variance = jnp.mean(centred * centred, axis=-1, keepdims=True)
        scaled = centred * lax.rsqrt(variance + 1e-06) * small[b, GAIN : GAIN + 1, :]
        return scaled.astype(jnp.bfloat16)

    def group(b, slots):
        normed = jnp.concatenate([convolve(b, g) for g in slots], axis=0)
        wide = jnp.concatenate(
            [small[b, UP_BIAS + q : UP_BIAS + q + 1, :] for q in range(hid // chans)], axis=1
        )
        hidden = jnp.dot(normed, ups[b], preferred_element_type=jnp.float32) + wide
        hidden = gelu(hidden).astype(jnp.bfloat16)
        branch = jnp.dot(hidden, downs[b], preferred_element_type=jnp.float32)
        branch = branch * small[b, SCALE : SCALE + 1, :]
        for n, g in enumerate(slots):
            at = pl.ds(pl.multiple_of(g * CELLS, CELLS), CELLS)
            alive = jnp.logical_or(g < live_count[0] - EDGE, g >= count - EDGE)
            state = win[b, at, :].astype(jnp.float32) + branch[n * CELLS : (n + 1) * CELLS]
            win[b + 1, at, :] = (state * jnp.where(alive, 1.0, 0.0)).astype(jnp.bfloat16)

    start_field.wait()
    halo(0, 0).start()
    halo(0, 1).start()
    own_up.wait()
    own_down.wait()
    for copy in to_partner():
        copy.start()

    @pl.when(core == 0)
    def _():
        for copy in to_pairs():
            copy.start()

    forward(0)

    def layer(b, carry):
        arrive(b)
        halo(b, 0).wait_recv()
        halo(b, 1).wait_recv()
        group(b, (count - 1, 0))

        @pl.when(b < blocks - 1)
        def _():
            halo(b + 1, 0).start()
            halo(b + 1, 1).start()
            forward(b + 1)

        @pl.when(jnp.logical_and(b == 0, core == 1))
        def _():
            for copy in to_pairs():
                copy.start()

        def rest(k, c):
            group(b, (2 * k + 1, 2 * k + 2))
            return c

        lax.fori_loop(0, (count - 2) // 2, rest, 0)

        s = b // BPS
        ends = lax.rem(b, BPS) == BPS - 1

        @pl.when(jnp.logical_and(ends, s != me))
        def _():
            send_result(s).start()

        @pl.when(jnp.logical_and(ends, s == me))
        def _():
            keep_result(s).start()

        return carry

    lax.fori_loop(0, blocks, layer, 0)

    for copy in to_partner() + to_pairs():
        copy.wait_send()

    def drain(b, carry):
        halo(b, 0).wait_send()
        halo(b, 1).wait_send()
        forwarded(b, lambda copy: copy.wait_send())
        return carry

    lax.fori_loop(0, blocks, drain, 0)
    keep_result(me).wait()
    for step in range(1, segments):
        send_result(lax.rem(me + step, segments)).wait_send()
    for step in range(1, segments):
        other = lax.rem(me + step, segments)
        pltpu.make_async_remote_copy(
            src_ref=result(0),
            dst_ref=out.at[other],
            send_sem=o_send.at[other],
            recv_sem=o_recv.at[other],
            device_id=(space, other),
            device_id_type=MESH,
        ).wait_recv()


def body(
    field,
    depth_kernel,
    depth_bias,
    norm_gain,
    up_weight,
    up_bias,
    down_weight,
    scale_exponent,
    live_count,
    neighbours,
    rotations,
):
    members, count = field.shape[:2]
    chans = field.shape[-1]
    hid = up_weight.shape[-1]
    segments = lax.axis_size("segment")
    devices = lax.axis_size("space")
    blocks = segments * BPS
    assert members == segments and segments % 2 == 0 and count % 2 == 0
    pairs = segments // 2
    smalls = -(-(UP_BIAS + hid // chans) // 8) * 8
    route = routing(neighbours, rotations)
    vmem = pl.BlockSpec(memory_space=pltpu.VMEM)
    smem = pl.BlockSpec(memory_space=pltpu.SMEM)
    hbm = pl.BlockSpec(memory_space=pl.ANY)
    dma = pltpu.SemaphoreType.DMA
    out = pl.pallas_call(
        functools.partial(kernel, segments, devices, blocks),
        out_shape=jax.ShapeDtypeStruct((members, count * CELLS, chans), jnp.bfloat16),
        in_specs=[hbm, vmem, vmem, vmem, hbm, vmem, hbm, vmem, smem, vmem],
        out_specs=hbm,
        scratch_shapes=[
            pltpu.VMEM((blocks + 1, (count + 2) * CELLS, chans), jnp.bfloat16),
            pltpu.VMEM((blocks, chans, hid), jnp.bfloat16),
            pltpu.VMEM((blocks, hid, chans), jnp.bfloat16),
            pltpu.VMEM((blocks, smalls, chans), jnp.float32),
            pltpu.VMEM((ROWS, chans), jnp.float32),
            dma((4,)),
            dma((BPS, 3 + 4 * (pairs - 1))),
            dma((3, blocks)),
            dma((blocks,)),
            dma((blocks, 2)),
            dma((blocks, 2)),
            dma((segments,)),
            dma((members,)),
        ],
        compiler_params=pltpu.CompilerParams(
            collective_id=0, has_side_effects=True, vmem_limit_bytes=40 * 2**20
        ),
    )(
        field.reshape(members, count * CELLS, chans),
        depth_kernel,
        depth_bias,
        norm_gain,
        up_weight,
        up_bias,
        down_weight,
        scale_exponent,
        live_count,
        route,
    )
    return out.reshape((1,) + field.shape)


def solution(mesh):
    in_specs = (
        P(None, "space", None, None, None),
        P("segment", None, None),
        P("segment", None),
        P("segment", None),
        P("segment", None, None),
        P("segment", None),
        P("segment", None, None),
        P("segment", None),
        P("space"),
        P("space", None),
        P("space", None),
    )
    out_specs = P("segment", None, "space", None, None, None)
    return jax.shard_map(body, mesh=mesh, in_specs=in_specs, out_specs=out_specs, check_vma=False)
```

```python
import functools

import jax
import jax.numpy as jnp
import numpy as np
from jax import lax
from jax.experimental import pallas as pl
from jax.experimental.pallas import tpu as pltpu
from jax.sharding import PartitionSpec as P

KS = 7
BPS = 2
EDGE = 1
MARGIN = KS // 2
PS = 8
CELLS = PS * PS
EXT = PS + 2 * MARGIN
PITCH = 15
ROWS = 224
LANES = 256
MESH = pl.DeviceIdType.MESH

BIAS = KS * KS
GAIN = BIAS + 1
SCALE = GAIN + 1
UP_BIAS = SCALE + 1


def tables():
    table = np.zeros((8, LANES), np.int32)
    table[0] = -1
    last = PS - 1
    for j in range(EXT):
        for i in range(EXT):
            band_i = 0 if i < MARGIN else (1 if i < MARGIN + PS else 2)
            band_j = 0 if j < MARGIN else (1 if j < MARGIN + PS else 2)
            u = (i + PS - MARGIN) % PS
            v = (j + PS - MARGIN) % PS
            r = j * PITCH + i
            table[0, r] = ((0, 1, 2), (3, 8, 4), (5, 6, 7))[band_i][band_j]
            turned = ((u, v), (v, last - u), (last - u, last - v), (last - v, u))
            for k, (p, q) in enumerate(turned):
                table[1 + k, r] = p * PS + q
    return table


def targets(neighbours, rotations, table, place, devices):
    count = neighbours.shape[0]
    local = neighbours - place * count
    following = lax.rem(place + 1, devices) * count
    slot = jnp.where(neighbours == following, count + 1, count)
    slot = jnp.where(jnp.logical_and(local >= 0, local < count), local, slot)
    slot = jnp.where(neighbours < 0, -1, slot)
    shape = (count, LANES)
    link = jnp.full(shape, -1, jnp.int32)
    turn = jnp.zeros(shape, jnp.int32)
    direction = jnp.broadcast_to(table[0:1, :], shape)
    for d in range(8):
        here = direction == d
        link = jnp.where(here, jnp.broadcast_to(slot[:, d : d + 1], shape), link)
        turn = jnp.where(here, jnp.broadcast_to(rotations[:, d : d + 1], shape), turn)
    link = jnp.where(direction == 8, lax.broadcasted_iota(jnp.int32, shape, 0), link)
    cell = jnp.broadcast_to(table[1:2, :], shape)
    for k in range(1, 4):
        cell = jnp.where(turn == k, jnp.broadcast_to(table[1 + k : 2 + k, :], shape), cell)
    return jnp.where(link < 0, -1, link * CELLS + cell)


def gelu(x):
    return 0.5 * x * (1.0 + lax.erf(x * np.float32(0.5**0.5)))


def kernel(
    segments,
    devices,
    blocks,
    field,
    taps,
    bias,
    gain,
    up,
    up_bias,
    down,
    scale,
    live_count,
    neighbours,
    rotations,
    table,
    out,
    win,
    ups,
    downs,
    small,
    route,
    ext,
    loc_sem,
    own_sem,
    w_recv,
    fwd_sem,
    h_send,
    h_recv,
    o_send,
    o_recv,
):
    space = lax.axis_index("space")
    me = lax.axis_index("segment")
    count = win.shape[1] // CELLS - 2
    rows = count * CELLS
    after = lax.rem(space + 1, devices)
    before = lax.rem(space + devices - 1, devices)
    core = lax.rem(me, 2)
    pair = me // 2
    partner = pair * 2 + (1 - core)
    pairs = segments // 2
    mine = me * BPS

    start_field = pltpu.make_async_copy(field.at[me], win.at[0, pl.ds(0, rows)], loc_sem.at[0])
    start_field.start()
    own_up = pltpu.make_async_copy(up, ups.at[pl.ds(mine, BPS)], loc_sem.at[1])
    own_up.start()
    own_down = pltpu.make_async_copy(down, downs.at[pl.ds(mine, BPS)], loc_sem.at[2])
    own_down.start()
    order = [count - 1, *range(count - 1)]
    half = 2 + (count - 2) // 2
    hid = up_bias.shape[1]
    chans = up.shape[1]
    for k in range(BPS):
        small[mine + k, 0 : KS * KS, :] = taps[:, k, :].astype(jnp.float32)
        small[mine + k, BIAS : BIAS + 1, :] = bias[k : k + 1, :].astype(jnp.float32)
        small[mine + k, GAIN : GAIN + 1, :] = gain[k : k + 1, :].astype(jnp.float32)
        small[mine + k, SCALE : SCALE + 1, :] = jnp.exp2(
            scale[k : k + 1, :].astype(jnp.float32) * 0.5
        )
        for q in range(hid // chans):
            small[mine + k, UP_BIAS + q : UP_BIAS + q + 1, :] = up_bias[
                k : k + 1, q * chans : (q + 1) * chans
            ].astype(jnp.float32)

    barrier = pltpu.get_barrier_semaphore()
    for step in range(1, segments):
        pl.semaphore_signal(
            barrier,
            inc=1,
            device_id=(space, lax.rem(me + step, segments)),
            device_id_type=MESH,
        )
    for side in (before, after):
        pl.semaphore_signal(barrier, inc=1, device_id=(side, me), device_id_type=MESH)
    pl.semaphore_wait(barrier, segments + 1)

    def halo(b, side):
        if side == 0:
            src = win.at[b, pl.ds(rows - CELLS, CELLS)]
            dst, to = win.at[b, pl.ds(rows, CELLS)], after
        else:
            src = win.at[b, pl.ds(0, CELLS)]
            dst, to = win.at[b, pl.ds(rows + CELLS, CELLS)], before
        return pltpu.make_async_remote_copy(
            src_ref=src,
            dst_ref=dst,
            send_sem=h_send.at[b, side],
            recv_sem=h_recv.at[b, side],
            device_id=(to, me),
            device_id_type=MESH,
        )

    def piece(kind, b, to, send_sem):
        ref = (small, ups, downs)[kind].at[b]
        return pltpu.make_async_remote_copy(
            src_ref=ref,
            dst_ref=ref,
            send_sem=send_sem,
            recv_sem=w_recv.at[kind, b],
            device_id=(space, to),
            device_id_type=MESH,
        )

    def to_partner():
        return [
            piece(kind, mine + k, partner, own_sem.at[k, kind])
            for k in range(BPS)
            for kind in range(3)
        ]

    def to_pairs(k):
        copies = []
        for step in range(1, pairs):
            other = lax.rem(pair + step, pairs) * 2
            at = 3 + (step - 1) * 4
            copies.append(piece(0, mine + k, other, own_sem.at[k, at]))
            copies.append(piece(0, mine + k, other + 1, own_sem.at[k, at + 1]))
            copies.append(piece(1, mine + k, other, own_sem.at[k, at + 2]))
            copies.append(piece(2, mine + k, other + 1, own_sem.at[k, at + 3]))
        return copies

    def forwarded(b, act):
        foreign = b // (2 * BPS) != pair

        @pl.when(jnp.logical_and(foreign, core == 0))
        def _():
            act(piece(1, b, partner, fwd_sem.at[b]))

        @pl.when(jnp.logical_and(foreign, core == 1))
        def _():
            act(piece(2, b, partner, fwd_sem.at[b]))

    def forward(b):
        def act(copy):
            copy.wait_recv()
            copy.start()

        forwarded(b, act)

    def arrive(b):
        owner = b // BPS
        foreign = b // (2 * BPS) != pair

        @pl.when(owner != me)
        def _():
            piece(0, b, partner, fwd_sem.at[b]).wait_recv()

        @pl.when(owner == partner)
        def _():
            piece(1, b, partner, fwd_sem.at[b]).wait_recv()
            piece(2, b, partner, fwd_sem.at[b]).wait_recv()

        @pl.when(jnp.logical_and(foreign, core == 0))
        def _():
            piece(2, b, partner, fwd_sem.at[b]).wait_recv()

        @pl.when(jnp.logical_and(foreign, core == 1))
        def _():
            piece(1, b, partner, fwd_sem.at[b]).wait_recv()

    def result(s):
        return win.at[BPS * (s + 1), pl.ds(0, rows)]

    def send_result(s):
        return pltpu.make_async_remote_copy(
            src_ref=result(s),
            dst_ref=out.at[me],
            send_sem=o_send.at[s],
            recv_sem=o_recv.at[me],
            device_id=(space, s),
            device_id_type=MESH,
        )

    def keep_result(s):
        return pltpu.make_async_copy(result(s), out.at[me], loc_sem.at[3])

    def build_route():
        target = targets(neighbours[...], rotations[...], table[...], space, devices)
        target = jnp.transpose(target.astype(jnp.float32))
        columns = lax.broadcasted_iota(jnp.int32, (ROWS, win.shape[1]), 1).astype(jnp.float32)
        for g in range(count):
            hit = jnp.broadcast_to(target[0:ROWS, g : g + 1], columns.shape) == columns
            at = order.index(g) * ROWS
            route[at : at + ROWS, :] = jnp.where(hit, 1.0, 0.0).astype(jnp.bfloat16)

    def gather(b, first, last):
        ext[first * ROWS : last * ROWS, :] = jnp.dot(
            route[first * ROWS : last * ROWS, :], win[b], preferred_element_type=jnp.float32
        )

    def convolve(b, n):
        total = jnp.broadcast_to(small[b, BIAS : BIAS + 1, :][None], (PS, PS, chans))
        for e in range(KS):
            base = n * ROWS + e * PITCH
            column = jnp.concatenate(
                [ext[pl.ds(base + i, PS, stride=PITCH), :][None] for i in range(EXT)], axis=0
            )
            for a in range(KS):
                tap = small[b, a * KS + e : a * KS + e + 1, :][None]
                total = total + column[a : a + PS] * tap
        total = total.reshape(CELLS, chans)
        centred = total - jnp.mean(total, axis=-1, keepdims=True)
        variance = jnp.mean(centred * centred, axis=-1, keepdims=True)
        scaled = centred * lax.rsqrt(variance + 1e-06) * small[b, GAIN : GAIN + 1, :]
        return scaled.astype(jnp.bfloat16)

    def group(b, first, last):
        normed = jnp.concatenate([convolve(b, n) for n in range(first, last)], axis=0)
        wide = jnp.concatenate(
            [small[b, UP_BIAS + q : UP_BIAS + q + 1, :] for q in range(hid // chans)], axis=1
        )
        hidden = jnp.dot(normed, ups[b], preferred_element_type=jnp.float32) + wide
        hidden = gelu(hidden).astype(jnp.bfloat16)
        branch = jnp.dot(hidden, downs[b], preferred_element_type=jnp.float32)
        branch = branch * small[b, SCALE : SCALE + 1, :]
        for n in range(first, last):
            g = order[n]
            at = pl.ds(g * CELLS, CELLS)
            alive = jnp.logical_or(g < live_count[0] - EDGE, g >= count - EDGE)
            here = branch[(n - first) * CELLS : (n - first + 1) * CELLS]
            state = win[b, at, :].astype(jnp.float32) + here
            win[b + 1, at, :] = (state * jnp.where(alive, 1.0, 0.0)).astype(jnp.bfloat16)

    start_field.wait()
    halo(0, 0).start()
    halo(0, 1).start()
    own_up.wait()
    own_down.wait()

    @pl.when(core == 0)
    def _():
        for copy in to_pairs(0):
            copy.start()

    for copy in to_partner():
        copy.start()
    build_route()
    forward(0)

    def layer(b, carry):
        arrive(b)
        halo(b, 0).wait_recv()
        halo(b, 1).wait_recv()
        gather(b, 0, 2)
        gather(b, 2, count)
        group(b, 0, 2)

        @pl.when(b < blocks - 1)
        def _():
            halo(b + 1, 0).start()
            halo(b + 1, 1).start()

        for k in range(BPS):
            for c in range(2):
                if k + c:

                    @pl.when(jnp.logical_and(b == k + 2 * c - 1, core == c))
                    def _():
                        for copy in to_pairs(k):
                            copy.start()

        group(b, 2, half)

        @pl.when(b < blocks - 1)
        def _():
            forward(b + 1)

        group(b, half, count)
        s = b // BPS
        ends = lax.rem(b, BPS) == BPS - 1

        @pl.when(jnp.logical_and(ends, s != me))
        def _():
            send_result(s).start()

        @pl.when(jnp.logical_and(ends, s == me))
        def _():
            keep_result(s).start()

        return carry

    lax.fori_loop(0, blocks, layer, 0)

    for copy in to_partner() + [copy for k in range(BPS) for copy in to_pairs(k)]:
        copy.wait_send()

    def drain(b, carry):
        halo(b, 0).wait_send()
        halo(b, 1).wait_send()
        forwarded(b, lambda copy: copy.wait_send())
        return carry

    lax.fori_loop(0, blocks, drain, 0)
    keep_result(me).wait()
    for step in range(1, segments):
        send_result(lax.rem(me + step, segments)).wait_send()
    for step in range(1, segments):
        other = lax.rem(me + step, segments)
        pltpu.make_async_remote_copy(
            src_ref=result(0),
            dst_ref=out.at[other],
            send_sem=o_send.at[other],
            recv_sem=o_recv.at[other],
            device_id=(space, other),
            device_id_type=MESH,
        ).wait_recv()


def body(
    field,
    depth_kernel,
    depth_bias,
    norm_gain,
    up_weight,
    up_bias,
    down_weight,
    scale_exponent,
    live_count,
    neighbours,
    rotations,
):
    members, count = field.shape[:2]
    chans = field.shape[-1]
    hid = up_weight.shape[-1]
    segments = lax.axis_size("segment")
    devices = lax.axis_size("space")
    blocks = segments * BPS
    assert members == segments and segments % 2 == 0 and count % 2 == 0
    pairs = segments // 2
    smalls = -(-(UP_BIAS + hid // chans) // 8) * 8
    vmem = pl.BlockSpec(memory_space=pltpu.VMEM)
    smem = pl.BlockSpec(memory_space=pltpu.SMEM)
    hbm = pl.BlockSpec(memory_space=pl.ANY)
    dma = pltpu.SemaphoreType.DMA
    out = pl.pallas_call(
        functools.partial(kernel, segments, devices, blocks),
        out_shape=jax.ShapeDtypeStruct((members, count * CELLS, chans), jnp.bfloat16),
        in_specs=[hbm, vmem, vmem, vmem, hbm, vmem, hbm, vmem, smem, vmem, vmem, vmem],
        out_specs=hbm,
        scratch_shapes=[
            pltpu.VMEM((blocks + 1, (count + 2) * CELLS, chans), jnp.bfloat16),
            pltpu.VMEM((blocks, chans, hid), jnp.bfloat16),
            pltpu.VMEM((blocks, hid, chans), jnp.bfloat16),
            pltpu.VMEM((blocks, smalls, chans), jnp.float32),
            pltpu.VMEM((count * ROWS, (count + 2) * CELLS), jnp.bfloat16),
            pltpu.VMEM((count * ROWS, chans), jnp.float32),
            dma((4,)),
            dma((BPS, 3 + 4 * (pairs - 1))),
            dma((3, blocks)),
            dma((blocks,)),
            dma((blocks, 2)),
            dma((blocks, 2)),
            dma((segments,)),
            dma((members,)),
        ],
        compiler_params=pltpu.CompilerParams(
            collective_id=0, has_side_effects=True, vmem_limit_bytes=40 * 2**20
        ),
    )(
        field.reshape(members, count * CELLS, chans),
        jnp.transpose(depth_kernel, (1, 0, 2)),
        depth_bias,
        norm_gain,
        up_weight,
        up_bias,
        down_weight,
        scale_exponent,
        live_count,
        neighbours,
        rotations,
        jnp.asarray(tables()),
    )
    return out.reshape((1,) + field.shape)


def solution(mesh):
    in_specs = (
        P(None, "space", None, None, None),
        P("segment", None, None),
        P("segment", None),
        P("segment", None),
        P("segment", None, None),
        P("segment", None),
        P("segment", None, None),
        P("segment", None),
        P("space"),
        P("space", None),
        P("space", None),
    )
    out_specs = P("segment", None, "space", None, None, None)
    return jax.shard_map(body, mesh=mesh, in_specs=in_specs, out_specs=out_specs, check_vma=False)
```
